512 devices in a mesh: rep: 64 (over y, z), fsdp: 8 (over x, core).
Axes of the slice: x: 4, y: 4, z: 16, core: 2. Of those that a mesh axis runs over, the one named last changes fastest.
Arguments:
- partial_grads: bfloat16 [64, 8, 64, 14336], P('rep', 'fsdp'), may hold values from -6 to 6
- momentum_old: float32 [64, 64, 14336], P('rep', None, 'fsdp'), may hold values from -6 to 6
- indices: int32 [64, 1, 224, 32], P('rep', None, 'fsdp'), may hold values from 0 to 4095, all different within a row
Outputs:
- new_momentum: float32 [64, 64, 14336], P('rep', None, 'fsdp')
- update: float32 [64, 14336], P(None, 'fsdp')
The draws below stay inside these ranges and needn't reach their ends.
Inputs may be any that keep to these rules, and one draw needn't show every extreme that they name: `indices`: the 32 numbers of one replica's tile are distinct.
All inputs are finite; a program needn't handle non-finite values.
Results may differ from the reference program's by a relative error of at most 0.0003.
Values sent between devices are 32-bit elements; how exact they have to be, the bound alone decides.
No kernel may reach another device: no remote copies, remote signals or barrier semaphores. Data moves between devices by JAX's collectives and lax.ppermute only.
A program may use at most 64 MiB of HBM per device.

```python
import jax
import jax.numpy as jnp
from jax import lax

WC = 14336
TILE = 64
K = 32
ROWS = 64
TR = 1
TC = 224
REPLICAS = 64
N_FSDP = 8


def strengthened(array, rng, source, target, blocks, factor):
    owner, partner = [(jnp.arange(array.shape[dim]) // (array.shape[dim] // blocks)).reshape([-1 if axis == dim else 1 for axis in range(array.ndim)]) for dim in (source, target)]
    chosen = jax.random.permutation(rng, blocks)[partner]
    strong = (owner == chosen) | (owner == (partner + blocks // 2) % blocks)
    return jnp.where(strong, factor * array, array)


def level_of(rng, dims, cuts, smallest, top_value):
    def one(position, parts):
        draws = jax.random.uniform(jax.random.fold_in(jax.random.fold_in(rng, 6), position), (parts,), jnp.float32, smallest / len(cuts), top_value / len(cuts))
        return jnp.repeat(jnp.exp(draws), dims[position] // parts).reshape((-1,) + (1,) * (len(dims) - position - 1))

    loudness = one(*cuts[0])
    for cut in cuts[1:]:
        loudness = loudness * one(*cut)
    return loudness


def distinct(key, rows, count, top, lift):
    sequence = jax.random.permutation(jax.random.fold_in(key, 1), count)
    favour = sequence
    for power in range(3):
        favour = favour * favour // count
    favour = favour * lift // count
    chance = jax.random.randint(jax.random.fold_in(key, 2), (rows, count), 0, 4096) + favour
    holders = jax.random.permutation(jax.random.fold_in(key, 3), rows)[jnp.arange(count) % rows]
    chance = jnp.where(jnp.arange(rows)[:, None] == holders[None, :], 1 << 14, chance)
    merit = chance * count + jnp.arange(count)
    return lax.top_k(merit.astype(jnp.int32), top)[1].astype(jnp.int32)


def centred(stream_key, extent, scale, limit, cuts=(), held_as=jnp.bfloat16):
    entries = scale * jax.random.normal(stream_key, extent, jnp.float32)
    if cuts:
        entries = entries * level_of(stream_key, extent, cuts, -0.22, 0.18)
    return jnp.clip(entries, -limit, limit).astype(held_as)


def bell_draw_with(own_key, shape, deviation, most, cuts, heavy, held_as=jnp.bfloat16):
    result = deviation * jax.random.normal(own_key, shape, jnp.float32)
    if cuts:
        result = result * level_of(own_key, shape, cuts, -0.22, 0.18)
    return jnp.clip(strengthened(result, jax.random.fold_in(own_key, 3), *heavy), -most, most).astype(held_as)


def setup_inputs(seed: int = 0) -> dict:
    splits = jax.random.split(jax.random.key(seed), 4)
    partial_grads = bell_draw_with(splits[0], (REPLICAS, N_FSDP, ROWS, WC), 1.0, 6.0, ((0, 64), (1, 8)), (1, 3, 8, 2.0))
    momentum_old = centred(splits[1], (REPLICAS, ROWS, WC), 1.0, 6.0, ((0, 64), (2, 8)), jnp.float32)
    indices = distinct(splits[2], REPLICAS * TR * TC, TILE * TILE, K, 0).reshape((REPLICAS, TR, TC, K))
    return {"partial_grads": partial_grads, "momentum_old": momentum_old, "indices": indices}


BETA_DECAY = 0.999

def dct_cosines():
    counter = jnp.arange(TILE, dtype=jnp.float32)
    scales = jnp.where(counter == 0, jnp.sqrt(1.0 / TILE), jnp.sqrt(2.0 / TILE)).astype(jnp.float32)
    angles = jnp.pi * (counter[None, :] + 0.5) * counter[:, None] / TILE
    return (scales[:, None] * jnp.cos(angles)).astype(jnp.float32)

def forward(source, cosines):
    rows_count, cols_count = source.shape
    shaped = source.reshape(rows_count // TILE, TILE, cols_count // TILE, TILE)
    mixed = jnp.einsum('kn,anbm->akbm', cosines, shaped, precision=lax.Precision.HIGHEST)
    mixed = jnp.einsum('lm,akbm->akbl', cosines, mixed, precision=lax.Precision.HIGHEST)
    return mixed.reshape(rows_count, cols_count)

def inverse(source, cosines):
    rows_count, cols_count = source.shape
    shaped = source.reshape(rows_count // TILE, TILE, cols_count // TILE, TILE)
    mixed = jnp.einsum('kn,akbl->anbl', cosines, shaped, precision=lax.Precision.HIGHEST)
    mixed = jnp.einsum('lm,anbl->anbm', cosines, mixed, precision=lax.Precision.HIGHEST)
    return mixed.reshape(rows_count, cols_count)

def positions(chosen, width):
    tile_row = jnp.arange(chosen.shape[-3], dtype=jnp.int32)[:, None, None]
    tile_col = jnp.arange(chosen.shape[-2], dtype=jnp.int32)[None, :, None]
    chosen = chosen.astype(jnp.int32)
    return ((tile_row * TILE + chosen // TILE) * width + tile_col * TILE + chosen % TILE).astype(jnp.int32)

def reference(partial_grads, momentum_old, indices):
    cosines = dct_cosines()

    def one_replica(running, inputs):
        partial_set, momentum_prev, chosen = inputs
        gradient = lax.optimization_barrier(jnp.sum(partial_set.astype(jnp.float32), axis=0))
        momentum = BETA_DECAY * momentum_prev + gradient
        coeffs = forward(momentum, cosines).reshape(-1)
        flat_spots = positions(chosen, WC).reshape(-1)
        selected = coeffs[flat_spots]
        own_dense = jnp.zeros_like(coeffs).at[flat_spots].set(selected)
        fresh = momentum - inverse(own_dense.reshape(ROWS, WC), cosines)
        return (running + own_dense, fresh)
    summed, new_momentum = lax.scan(one_replica, jnp.zeros((ROWS * WC,), jnp.float32), (partial_grads, momentum_old, indices))
    update = inverse(summed.reshape(ROWS, WC), cosines)
    return (new_momentum, update)
```

```python
import jax
import jax.numpy as jnp
from jax import lax
from jax.sharding import PartitionSpec as P

TILE = 64


BETA_DECAY = 0.999


def dct_cosines():
    counter = jnp.arange(TILE, dtype=jnp.float32)
    scales = jnp.where(counter == 0, jnp.sqrt(1.0 / TILE), jnp.sqrt(2.0 / TILE)).astype(jnp.float32)
    angles = jnp.pi * (counter[None, :] + 0.5) * counter[:, None] / TILE
    return scales[:, None] * jnp.cos(angles)


def forward(source, cosines):
    rows_count, cols_count = source.shape
    shaped = source.reshape(rows_count // TILE, TILE, cols_count // TILE, TILE)
    mixed = jnp.einsum("kn,anbm->akbm", cosines, shaped, precision=lax.Precision.HIGHEST)
    mixed = jnp.einsum("lm,akbm->akbl", cosines, mixed, precision=lax.Precision.HIGHEST)
    return mixed.reshape(rows_count, cols_count)


def inverse(source, cosines):
    rows_count, cols_count = source.shape
    shaped = source.reshape(rows_count // TILE, TILE, cols_count // TILE, TILE)
    mixed = jnp.einsum("kn,akbl->anbl", cosines, shaped, precision=lax.Precision.HIGHEST)
    mixed = jnp.einsum("lm,anbl->anbm", cosines, mixed, precision=lax.Precision.HIGHEST)
    return mixed.reshape(rows_count, cols_count)


def to_tiles(matrix):
    rows_count, cols_count = matrix.shape
    return matrix.reshape(rows_count // TILE, TILE, cols_count // TILE, TILE).transpose(0, 2, 1, 3)


def from_tiles(blocks):
    tile_rows, tile_cols = (blocks.shape[0], blocks.shape[1])
    return blocks.transpose(0, 2, 1, 3).reshape(tile_rows * TILE, tile_cols * TILE)


def hot_pair(numbers):
    counter = jnp.arange(TILE, dtype=jnp.int32)
    numbers = numbers.astype(jnp.int32)
    row_hot = ((numbers // TILE)[..., None] == counter).astype(jnp.float32)
    col_hot = ((numbers % TILE)[..., None] == counter).astype(jnp.float32)
    return (row_hot, col_hot)


def pick_own(coeff_matrix, numbers):
    blocks = to_tiles(coeff_matrix)
    row_hot, col_hot = hot_pair(numbers)
    along = jnp.einsum("abkm,abjm->abjk", blocks, col_hot, precision=lax.Precision.HIGHEST)
    selected = jnp.sum(along * row_hot, axis=-1)
    keep_mask = jnp.einsum("abjk,abjm->abkm", row_hot, col_hot, precision=lax.Precision.HIGHEST)
    own_dense = from_tiles(blocks * keep_mask)
    return (selected, own_dense)


def gather_over_rep(block):
    copies = jnp.broadcast_to(block, (64,) + block.shape[1:])
    return lax.all_to_all(copies, "rep", 0, 0, tiled=True)


def on_device(partial_grads, momentum_old, indices):
    cosines = dct_cosines()
    numbers = indices[0]
    gradient = lax.psum_scatter(
        partial_grads.astype(jnp.float32), "fsdp", scatter_dimension=3, tiled=True
    )
    momentum = BETA_DECAY * momentum_old[0] + gradient[0, 0]
    coeffs = forward(momentum, cosines)
    selected, own_dense = pick_own(coeffs, numbers)
    fresh = momentum - inverse(own_dense, cosines)
    sent_values = selected
    sent_numbers = indices.astype(jnp.float32)
    values = gather_over_rep(sent_values[:, None])
    sent = gather_over_rep(sent_numbers)
    row_hot, col_hot = hot_pair(sent)
    weighted = values[..., None] * row_hot
    summed_tiles = jnp.einsum(
        "pabjk,pabjm->abkm", weighted, col_hot, precision=lax.Precision.HIGHEST
    )
    summed = from_tiles(summed_tiles)
    update = inverse(summed, cosines)
    return (fresh[None], update)


def solution(mesh):
    in_specs = (P("rep", "fsdp", None, None), P("rep", None, "fsdp"), P("rep", None, "fsdp", None))
    out_specs = (P("rep", None, "fsdp"), P(None, "fsdp"))
    return jax.shard_map(
        on_device, mesh=mesh, in_specs=in_specs, out_specs=out_specs, check_vma=False
    )
```

```python
import functools

import jax
import jax.numpy as jnp
import ml_dtypes
import numpy as np
from jax import lax
from jax.experimental import pallas as pl
from jax.experimental.pallas import tpu as pltpu
from jax.sharding import PartitionSpec as P

TILE = 64
KEPT = 32
LANES = 128
GROUP = LANES // KEPT
WIDE = GROUP * TILE
BETA_DECAY = 0.999
F32 = jnp.float32
BF16 = jnp.bfloat16


def split_table(table):
    high = table.astype(ml_dtypes.bfloat16)
    low = (table - high.astype(np.float64)).astype(ml_dtypes.bfloat16)
    return high, low


def dct_cosines():
    counter = np.arange(TILE)
    scales = np.where(counter == 0, np.sqrt(1.0 / TILE), np.sqrt(2.0 / TILE))
    return scales[:, None] * np.cos(np.pi * (counter[None, :] + 0.5) * counter[:, None] / TILE)


def pick_table():
    high, low = split_table(dct_cosines().T)
    zero = np.zeros_like(high)
    return np.block([[high, zero], [low, zero], [zero, high], [zero, low]])


def wide_table():
    high, low = split_table(dct_cosines())
    eye = np.eye(GROUP)
    return np.concatenate([np.kron(eye, high.astype(np.float32)), np.kron(eye, low.astype(np.float32))], 0).astype(
        ml_dtypes.bfloat16
    )


def tall_table():
    high, low = split_table(dct_cosines().T)
    return np.concatenate([high, low, high], 1)


def halves(value):
    high = value.astype(BF16)
    return high, (value - high.astype(F32)).astype(BF16)


def cosine_rows(table, row):
    counter = lax.broadcasted_iota(jnp.int32, (TILE, LANES), 0)
    hot = jnp.concatenate([counter == (row >> 6), counter == (row & 63)], 0)
    both = jnp.dot(table, jnp.where(hot, 1.0, 0.0).astype(BF16), preferred_element_type=F32)
    down = both[:TILE] + both[TILE : 2 * TILE]
    own = (lax.broadcasted_iota(jnp.int32, (WIDE, LANES), 0) // TILE) == (
        lax.broadcasted_iota(jnp.int32, (WIDE, LANES), 1) // KEPT
    )
    high = jnp.concatenate([both[2 * TILE : 3 * TILE]] * GROUP, 0)
    low = jnp.concatenate([both[3 * TILE :]] * GROUP, 0)
    high = jnp.where(own, high, 0.0).astype(BF16)
    low = jnp.where(own, low, 0.0).astype(BF16)
    return down, jnp.concatenate([high, low], 1)


def picked(source, down, across):
    mixed = jnp.dot(source, across, preferred_element_type=F32)
    return jnp.sum((mixed[:, :LANES] + mixed[:, LANES:]) * down, axis=0, keepdims=True)


def pick_kernel(table_ref, grads_ref, numbers_ref, momentum_ref, own_numbers_ref, values_ref, wide_ref, own_ref):
    groups = numbers_ref.shape[1]
    wide_ref[0] = grads_ref[...].astype(F32)
    for group in range(groups):
        columns = slice(group * WIDE, (group + 1) * WIDE)
        down, across = cosine_rows(table_ref[...], numbers_ref[0, group : group + 1, :])
        values_ref[0, group : group + 1, :] = picked(grads_ref[:, columns], down, across)

    @pl.when(pl.program_id(0) == 0)
    def _():
        for group in range(groups):
            columns = slice(group * WIDE, (group + 1) * WIDE)
            down, across = cosine_rows(table_ref[...], own_numbers_ref[group : group + 1, :])
            high, low = halves(momentum_ref[:, columns])
            own_ref[group : group + 1, :] = BETA_DECAY * (picked(high, down, across) + picked(low, down, across))


def pick(grads, numbers, momentum, own_numbers):
    parts, groups, _ = numbers.shape
    rows, columns = momentum.shape
    return pl.pallas_call(
        pick_kernel,
        grid=(parts,),
        in_specs=[
            pl.BlockSpec((4 * TILE, LANES), lambda i: (0, 0)),
            pl.BlockSpec((rows, columns), lambda i: (0, i)),
            pl.BlockSpec((1, groups, LANES), lambda i: (i, 0, 0)),
            pl.BlockSpec((rows, columns), lambda i: (0, 0)),
            pl.BlockSpec((groups, LANES), lambda i: (0, 0)),
        ],
        out_specs=[
            pl.BlockSpec((1, groups, LANES), lambda i: (i, 0, 0)),
            pl.BlockSpec((1, rows, columns), lambda i: (i, 0, 0)),
            pl.BlockSpec((groups, LANES), lambda i: (0, 0)),
        ],
        out_shape=[
            jax.ShapeDtypeStruct((parts, groups, LANES), F32),
            jax.ShapeDtypeStruct((parts, rows, columns), F32),
            jax.ShapeDtypeStruct((groups, LANES), F32),
        ],
        compiler_params=pltpu.CompilerParams(vmem_limit_bytes=32 * 2**20),
        name="pick",
    )(jnp.asarray(pick_table()), grads, numbers, momentum, own_numbers)


def parts_of(numbers, values):
    numbers = numbers.astype(jnp.int32)
    lane_tile = lax.broadcasted_iota(jnp.int32, numbers.shape, numbers.ndim - 1) // KEPT
    high = values.astype(BF16).astype(F32)
    return (numbers >> 6).astype(F32), ((numbers & 63) + lane_tile * TILE).astype(F32), high, values - high


def hot_rows(row, column, high, low):
    def spread(value, count):
        return jnp.broadcast_to(value, (count, LANES)).astype(BF16)

    counter = lax.broadcasted_iota(jnp.int32, (WIDE, LANES), 0).astype(F32).astype(BF16)
    zero = jnp.zeros((), BF16)
    at_row = counter[:TILE] == spread(row, TILE)
    at_column = counter == spread(column, WIDE)
    weighted = jnp.concatenate(
        [jnp.where(at_row, spread(high, TILE), zero), jnp.where(at_row, spread(low, TILE), zero)], 0
    )
    return weighted, jnp.where(at_column, jnp.ones((), BF16), zero)


NT = (((1,), (1,)), ((), ()))


def back(dense, tall, wide):
    high, low = halves(dense)
    half = jnp.dot(tall, jnp.concatenate([high, high, low], 0), preferred_element_type=F32)
    high, low = halves(half)
    both = jnp.dot(jnp.concatenate([high, low], 0), wide[:WIDE], preferred_element_type=F32)
    return both[:TILE] + both[TILE:] + jnp.dot(high, wide[WIDE:], preferred_element_type=F32)


def spread_kernel(
    tall_ref, wide_ref, sent_ref, own_ref, momentum_ref, grad_ref, fresh_ref, update_ref, rows_ref, left_ref, right_ref
):
    replicas = sent_ref.shape[0]
    groups = momentum_ref.shape[1] // WIDE
    batch = left_ref.shape[2] // LANES
    step = 8
    values = sent_ref[:, :8, :]
    numbers = sent_ref[:, 8:, :]
    for part, value in enumerate(parts_of(numbers, values)):
        rows_ref[part] = value

    for group in range(groups):
        columns = slice(group * WIDE, (group + 1) * WIDE)
        total = jnp.zeros((2 * TILE, WIDE), F32)
        for first in range(0, replicas, batch):
            slot = (first // batch) % 2
            for replica in range(batch):
                lanes = slice(replica * LANES, (replica + 1) * LANES)
                left, right = hot_rows(*(rows_ref[part, first + replica, group : group + 1, :] for part in range(4)))
                left_ref[slot, :, lanes] = left
                right_ref[slot, :, lanes] = right
            total += lax.dot_general(left_ref[slot], right_ref[slot], NT, preferred_element_type=F32)
        update_ref[:, columns] = back(total[:TILE] + total[TILE:], tall_ref[...], wide_ref[...])

        own = parts_of(own_ref[8 + group : 9 + group, :], own_ref[group : group + 1, :])
        left, right = hot_rows(*own)
        dense = lax.dot_general(left, right, NT, preferred_element_type=F32)
        shared = back(dense[:TILE] + dense[TILE:], tall_ref[...], wide_ref[...])
        fresh_ref[:, columns] = BETA_DECAY * momentum_ref[:, columns] + grad_ref[:, columns] - shared


def spread(sent, own, momentum, grad, batch=8):
    rows, columns = momentum.shape
    replicas = sent.shape[0]
    return pl.pallas_call(
        spread_kernel,
        out_shape=[jax.ShapeDtypeStruct((rows, columns), F32)] * 2,
        scratch_shapes=[
            pltpu.VMEM((4, replicas, 8, LANES), F32),
            pltpu.VMEM((2, 2 * TILE, batch * LANES), BF16),
            pltpu.VMEM((2, WIDE, batch * LANES), BF16),
        ],
        compiler_params=pltpu.CompilerParams(vmem_limit_bytes=32 * 2**20),
        name="spread",
    )(jnp.asarray(tall_table()), jnp.asarray(wide_table()), sent, own, momentum, grad)


FSDP = ("x", "core")


def copies_to(block, count, axis):
    return lax.all_to_all(jnp.broadcast_to(block[None], (count,) + block.shape), axis, 0, 0, tiled=True)


def on_device(partial_grads, momentum_old, indices):
    groups = indices.shape[2] // GROUP
    momentum = momentum_old[0]
    own_numbers = indices.reshape(groups, LANES)
    parts = lax.axis_size(FSDP)
    numbers = copies_to(own_numbers, parts, FSDP)
    values, wide, own_part = pick(partial_grads[0, 0], numbers, momentum, own_numbers)
    grad = lax.psum_scatter(wide, FSDP, scatter_dimension=0, tiled=True)[0]
    values = lax.all_to_all(values, FSDP, 0, 0, tiled=True)
    selected = jnp.sum(values, axis=0) + own_part
    own = jnp.concatenate(
        [jnp.pad(part, ((0, 8 - groups), (0, 0))) for part in (selected, own_numbers.astype(F32))], 0
    )
    sent = copies_to(own, lax.axis_size("z"), "z")
    sent = copies_to(sent, lax.axis_size("y"), "y").reshape(-1, 16, LANES)
    fresh, update = spread(sent, own, momentum, grad)
    return fresh[None], update


def solution(mesh):
    fine = jax.sharding.Mesh(mesh.devices.reshape(4, 16, 4, 2), ("y", "z", "x", "core"))
    rep = ("y", "z")
    in_specs = (P(rep, FSDP, None, None), P(rep, None, FSDP), P(rep, None, FSDP, None))
    out_specs = (P(rep, None, FSDP), P(None, FSDP))
    return jax.shard_map(on_device, mesh=fine, in_specs=in_specs, out_specs=out_specs, check_vma=False)
```

```python
import functools

import jax
import jax.numpy as jnp
import ml_dtypes
import numpy as np
from jax import lax
from jax.experimental import pallas as pl
from jax.experimental.pallas import tpu as pltpu
from jax.sharding import PartitionSpec as P

TILE = 64
KEPT = 32
LANES = 128
GROUP = LANES // KEPT
WIDE = GROUP * TILE
BETA_DECAY = 0.999
WHOLE_VMEM = 60 * 2**20
F32 = jnp.float32
BF16 = jnp.bfloat16


def split_table(table):
    high = table.astype(ml_dtypes.bfloat16)
    low = (table - high.astype(np.float64)).astype(ml_dtypes.bfloat16)
    return high, low


def dct_cosines():
    counter = np.arange(TILE)
    scales = np.where(counter == 0, np.sqrt(1.0 / TILE), np.sqrt(2.0 / TILE))
    return scales[:, None] * np.cos(np.pi * (counter[None, :] + 0.5) * counter[:, None] / TILE)


def pick_table():
    high, low = split_table(dct_cosines().T)
    zero = np.zeros_like(high)
    return np.block([[high, zero], [low, zero], [zero, high], [zero, low]])


def wide_table():
    high, low = split_table(dct_cosines())
    eye = np.eye(GROUP)
    return np.concatenate([np.kron(eye, high.astype(np.float32)), np.kron(eye, low.astype(np.float32))], 0).astype(
        ml_dtypes.bfloat16
    )


def tall_table():
    high, low = split_table(dct_cosines().T)
    return np.concatenate([high, low, high], 1)


def halves(value):
    high = value.astype(BF16)
    return high, (value - high.astype(F32)).astype(BF16)


def cosine_rows(table, row):
    counter = lax.broadcasted_iota(jnp.int32, (TILE, LANES), 0)
    hot = jnp.concatenate([counter == (row >> 6), counter == (row & 63)], 0)
    both = jnp.dot(table, jnp.where(hot, 1.0, 0.0).astype(BF16), preferred_element_type=F32)
    down = both[:TILE] + both[TILE : 2 * TILE]
    own = (lax.broadcasted_iota(jnp.int32, (WIDE, LANES), 0) // TILE) == (
        lax.broadcasted_iota(jnp.int32, (WIDE, LANES), 1) // KEPT
    )
    high = jnp.concatenate([both[2 * TILE : 3 * TILE]] * GROUP, 0)
    low = jnp.concatenate([both[3 * TILE :]] * GROUP, 0)
    high = jnp.where(own, high, 0.0).astype(BF16)
    low = jnp.where(own, low, 0.0).astype(BF16)
    return down, jnp.concatenate([high, low], 1)


def picked(source, down, across):
    mixed = jnp.dot(source, across, preferred_element_type=F32)
    return jnp.sum((mixed[:, :LANES] + mixed[:, LANES:]) * down, axis=0, keepdims=True)


def pick_kernel(table_ref, grads_ref, numbers_ref, values_ref):
    groups = numbers_ref.shape[1]
    for group in range(groups):
        columns = slice(group * WIDE, (group + 1) * WIDE)
        down, across = cosine_rows(table_ref[...], numbers_ref[0, group : group + 1, :])
        values_ref[0, group : group + 1, :] = picked(grads_ref[:, columns], down, across)


def own_kernel(table_ref, momentum_ref, numbers_ref, own_ref):
    for group in range(numbers_ref.shape[0]):
        columns = slice(group * WIDE, (group + 1) * WIDE)
        down, across = cosine_rows(table_ref[...], numbers_ref[group : group + 1, :])
        high, low = halves(momentum_ref[:, columns])
        own_ref[group : group + 1, :] = BETA_DECAY * (picked(high, down, across) + picked(low, down, across))


def pick_own(momentum, numbers):
    return pl.pallas_call(
        own_kernel,
        out_shape=jax.ShapeDtypeStruct(numbers.shape, F32),
        cost_estimate=pl.CostEstimate(flops=4 * 10**8, bytes_accessed=2**19, transcendentals=0),
        compiler_params=pltpu.CompilerParams(vmem_limit_bytes=32 * 2**20),
        name="pick_own",
    )(jnp.asarray(pick_table()), momentum, numbers)


def pick(grads, numbers):
    parts, groups, _ = numbers.shape
    rows, columns = grads.shape
    return pl.pallas_call(
        pick_kernel,
        grid=(parts,),
        in_specs=[
            pl.BlockSpec((4 * TILE, LANES), lambda i: (0, 0)),
            pl.BlockSpec((rows, columns // parts), lambda i: (0, i)),
            pl.BlockSpec((1, groups, LANES), lambda i: (i, 0, 0)),
        ],
        out_specs=pl.BlockSpec((1, groups, LANES), lambda i: (i, 0, 0)),
        out_shape=jax.ShapeDtypeStruct((parts, groups, LANES), F32),
        cost_estimate=pl.CostEstimate(flops=2 * 10**9, bytes_accessed=2**21, transcendentals=0),
        compiler_params=pltpu.CompilerParams(vmem_limit_bytes=WHOLE_VMEM),
        name="pick",
    )(jnp.asarray(pick_table()), grads, numbers)


def parts_of(numbers, values):
    numbers = numbers.astype(jnp.int32)
    high = values.astype(BF16).astype(F32)
    return (numbers >> 6).astype(F32), (numbers & 63).astype(F32), high, values - high


SLAB = 16


def one_hots(row, column, high, low):
    row, column, high, low = (jnp.broadcast_to(part, (SLAB, LANES)).astype(BF16) for part in (row, column, high, low))
    counter = lax.broadcasted_iota(jnp.int32, (SLAB, LANES), 0).astype(F32).astype(BF16)
    counters = [counter + jnp.asarray(first, BF16) for first in range(0, TILE, SLAB)]
    zero, one = jnp.zeros((SLAB, LANES), BF16), jnp.ones((SLAB, LANES), BF16)
    at_row = [row == counter for counter in counters]
    weighted = [jnp.where(at, part, zero) for part in (high, low) for at in at_row]
    return jnp.concatenate(weighted, 0), jnp.concatenate([jnp.where(column == at, one, zero) for at in counters], 0)


NT = (((1,), (1,)), ((), ()))


def back(dense, tall, wide):
    high, low = halves(dense)
    half = jnp.dot(tall, jnp.concatenate([high, high, low], 0), preferred_element_type=F32)
    high, low = halves(half)
    both = jnp.dot(jnp.concatenate([high, low], 0), wide[:WIDE], preferred_element_type=F32)
    return both[:TILE] + both[TILE:] + jnp.dot(high, wide[WIDE:], preferred_element_type=F32)


def by_tile(block):
    lane_part = lax.broadcasted_iota(jnp.int32, (SLAB, LANES), 1) // KEPT
    rows = [block[SLAB * part : SLAB * (part + 1)] for part in range(GROUP)]
    tiles = []
    for tile in range(GROUP):
        moved = [pltpu.roll(rows[p], (KEPT * (p - tile)) % LANES, 1) if p != tile else rows[p] for p in range(GROUP)]
        total = moved[0]
        for part in range(1, GROUP):
            total = jnp.where(lane_part == part, moved[part], total)
        tiles.append(total)
    return tiles


def scattered(rows_ref, count):
    made = [one_hots(*(rows_ref[part, row : row + 1, :] for part in range(4))) for row in range(count)]
    total = lax.dot_general(
        jnp.concatenate([left for left, _ in made], 1),
        jnp.concatenate([right for _, right in made], 1),
        NT,
        preferred_element_type=F32,
    )
    return total[:TILE] + total[TILE:]


def spread_kernel(tall_ref, wide_ref, sent_ref, update_ref, rows_ref):
    groups = update_ref.shape[1] // WIDE
    replicas = sent_ref.shape[0] // SLAB
    for group in range(groups):
        values = by_tile(sent_ref[pl.ds(group, replicas, stride=SLAB), :])
        numbers = by_tile(sent_ref[pl.ds(SLAB // 2 + group, replicas, stride=SLAB), :])
        for tile in range(GROUP):
            for part, value in enumerate(parts_of(numbers[tile], values[tile])):
                rows_ref[group % 2, tile, part] = value
        dense = [scattered(rows_ref.at[group % 2, tile], SLAB) for tile in range(GROUP)]
        update_ref[:, group * WIDE : (group + 1) * WIDE] = back(
            jnp.concatenate(dense, 1), tall_ref[...], wide_ref[...]
        )


def spread(sent, columns):
    return pl.pallas_call(
        spread_kernel,
        out_shape=jax.ShapeDtypeStruct((TILE, columns), F32),
        scratch_shapes=[pltpu.VMEM((2, GROUP, 4, SLAB, LANES), F32)],
        compiler_params=pltpu.CompilerParams(vmem_limit_bytes=32 * 2**20),
        cost_estimate=pl.CostEstimate(flops=2 * 10**9, bytes_accessed=2**20, transcendentals=0),
        name="spread",
    )(jnp.asarray(tall_table()), jnp.asarray(wide_table()), sent.reshape(-1, LANES))


def shared_kernel(tall_ref, wide_ref, values_ref, numbers_ref, momentum_ref, left_ref):
    groups = values_ref.shape[0]
    lane_tile = lax.broadcasted_iota(jnp.int32, (1, LANES), 1) // KEPT
    for group in range(groups):
        columns = slice(group * WIDE, (group + 1) * WIDE)
        row, column, high, low = parts_of(numbers_ref[group : group + 1, :], values_ref[group : group + 1, :])
        weighted, hot = one_hots(row, column, high, low)
        hot = jnp.concatenate([jnp.where(lane_tile == tile, hot, jnp.zeros((), BF16)) for tile in range(GROUP)], 0)
        dense = lax.dot_general(weighted, hot, NT, preferred_element_type=F32)
        dense = dense[:TILE] + dense[TILE:]
        left_ref[:, columns] = BETA_DECAY * momentum_ref[:, columns] - back(dense, tall_ref[...], wide_ref[...])


def shared(values, numbers, momentum):
    return pl.pallas_call(
        shared_kernel,
        out_shape=jax.ShapeDtypeStruct(momentum.shape, F32),
        compiler_params=pltpu.CompilerParams(vmem_limit_bytes=32 * 2**20),
        cost_estimate=pl.CostEstimate(flops=4 * 10**8, bytes_accessed=2**20, transcendentals=0),
        name="shared",
    )(jnp.asarray(tall_table()), jnp.asarray(wide_table()), values, numbers, momentum)


FSDP = ("x", "core")


def copies_to(block, axis):
    count = lax.axis_size(axis)
    return lax.all_to_all(jnp.broadcast_to(block[None], (count,) + block.shape), axis, 0, 0, tiled=True)


def core_blocks(grads, core, columns):
    blocks = [grads[:, first : first + columns] for first in range(0, grads.shape[1], columns)]
    pairs = zip(blocks[::2], blocks[1::2], strict=True)
    return jnp.stack([jnp.where(core == 0, even, odd).astype(F32) for even, odd in pairs])


def others_of(blocks):
    count = blocks.shape[0]
    chip = lax.axis_index("x")
    taken = []
    for step in (2, 1, 3, 0):
        block = lax.dynamic_index_in_dim(blocks, (chip + step) % count, 0, keepdims=False)
        if step:
            block = lax.ppermute(block, "x", [(i, (i + step) % count) for i in range(count)])
        taken.append(block)
    return taken


def on_device(partial_grads, momentum_old, indices):
    groups = indices.shape[2] // GROUP
    grads, momentum = partial_grads[0, 0], momentum_old[0]
    columns = momentum.shape[1]
    core = lax.axis_index("core")
    own_numbers = indices.reshape(groups, LANES)
    numbers = copies_to(own_numbers, FSDP)
    other = core_blocks(grads, 1 - core, columns)
    own_part = pick_own(momentum, own_numbers)
    numbers, other, own_part = lax.optimization_barrier((numbers, other, own_part))
    arrived = lax.ppermute(other, "core", [(0, 1), (1, 0)])
    values = pick(grads, numbers)
    values = lax.all_to_all(values, FSDP, 0, 0, tiled=True)
    chip_sums = core_blocks(grads, core, columns) + arrived
    values, chip_sums = lax.optimization_barrier((values, chip_sums))
    parts = others_of(chip_sums)
    selected = jnp.sum(values, axis=0) + own_part
    own = jnp.concatenate(
        [jnp.pad(part, ((0, SLAB // 2 - groups), (0, 0))) for part in (selected, own_numbers.astype(F32))], 0
    )
    sent = copies_to(own, "z")
    left = shared(selected, own_numbers, momentum)
    sent, left = lax.optimization_barrier((sent, left))
    sent = copies_to(sent, "y")
    update = spread(sent, columns)
    fresh = left + sum(parts)
    return fresh[None], update


def solution(mesh):
    fine = jax.sharding.Mesh(mesh.devices.reshape(4, 16, 4, 2), ("y", "z", "x", "core"))
    rep = ("y", "z")
    in_specs = (P(rep, FSDP, None, None), P(rep, None, FSDP), P(rep, None, FSDP, None))
    out_specs = (P(rep, None, FSDP), P(None, FSDP))
    return jax.shard_map(on_device, mesh=fine, in_specs=in_specs, out_specs=out_specs, check_vma=False)
```

```python
import functools

import jax
import jax.numpy as jnp
import ml_dtypes
import numpy as np
from jax import lax
from jax.experimental import pallas as pl
from jax.experimental.pallas import tpu as pltpu
from jax.sharding import PartitionSpec as P

TILE = 64
KEPT = 32
LANES = 128
GROUP = LANES // KEPT
WIDE = GROUP * TILE
BETA_DECAY = 0.999
FAR_RUNS = 4
F32 = jnp.float32
BF16 = jnp.bfloat16


def split_table(table):
    high = table.astype(ml_dtypes.bfloat16)
    low = (table - high.astype(np.float64)).astype(ml_dtypes.bfloat16)
    return high, low


def dct_cosines():
    counter = np.arange(TILE)
    scales = np.where(counter == 0, np.sqrt(1.0 / TILE), np.sqrt(2.0 / TILE))
    return scales[:, None] * np.cos(np.pi * (counter[None, :] + 0.5) * counter[:, None] / TILE)


def pick_table():
    high, low = split_table(dct_cosines().T)
    zero = np.zeros_like(high)
    return np.block([[high, zero], [low, zero], [zero, high], [zero, low]])


def wide_table():
    high, low = split_table(dct_cosines())
    eye = np.eye(GROUP)
    return np.concatenate([np.kron(eye, high.astype(np.float32)), np.kron(eye, low.astype(np.float32))], 0).astype(
        ml_dtypes.bfloat16
    )


def tall_table():
    high, low = split_table(dct_cosines().T)
    return np.concatenate([high, low, high], 1)


def halves(value):
    high = value.astype(BF16)
    return high, (value - high.astype(F32)).astype(BF16)


def cosine_rows(table, row):
    counter = lax.broadcasted_iota(jnp.int32, (TILE, LANES), 0)
    hot = jnp.concatenate([counter == (row >> 6), counter == (row & 63)], 0)
    both = jnp.dot(table, jnp.where(hot, 1.0, 0.0).astype(BF16), preferred_element_type=F32)
    down = both[:TILE] + both[TILE : 2 * TILE]
    own = (lax.broadcasted_iota(jnp.int32, (WIDE, LANES), 0) // TILE) == (
        lax.broadcasted_iota(jnp.int32, (WIDE, LANES), 1) // KEPT
    )
    high = jnp.concatenate([both[2 * TILE : 3 * TILE]] * GROUP, 0)
    low = jnp.concatenate([both[3 * TILE :]] * GROUP, 0)
    high = jnp.where(own, high, 0.0).astype(BF16)
    low = jnp.where(own, low, 0.0).astype(BF16)
    return down, jnp.concatenate([high, low], 1)


def picked(source, down, across):
    mixed = jnp.dot(source, across, preferred_element_type=F32)
    return jnp.sum((mixed[:, :LANES] + mixed[:, LANES:]) * down, axis=0, keepdims=True)


def pick_kernel(table_ref, grads_ref, numbers_ref, values_ref):
    parts, groups, _ = numbers_ref.shape
    for part in range(parts):
        for group in range(groups):
            first = (part * groups + group) * WIDE
            down, across = cosine_rows(table_ref[...], numbers_ref[part, group : group + 1, :])
            values_ref[part, group : group + 1, :] = picked(grads_ref[:, first : first + WIDE], down, across)


def own_kernel(table_ref, momentum_ref, numbers_ref, own_ref):
    for group in range(numbers_ref.shape[0]):
        columns = slice(group * WIDE, (group + 1) * WIDE)
        down, across = cosine_rows(table_ref[...], numbers_ref[group : group + 1, :])
        high, low = halves(momentum_ref[:, columns])
        own_ref[group : group + 1, :] = BETA_DECAY * (picked(high, down, across) + picked(low, down, across))


def pick_own(momentum, numbers):
    return pl.pallas_call(
        own_kernel,
        out_shape=jax.ShapeDtypeStruct(numbers.shape, F32),
        cost_estimate=pl.CostEstimate(flops=4 * 10**8, bytes_accessed=2**19, transcendentals=0),
        compiler_params=pltpu.CompilerParams(vmem_limit_bytes=32 * 2**20),
        name="pick_own",
    )(jnp.asarray(pick_table()), momentum, numbers)


def pick(grads, numbers):
    return pl.pallas_call(
        pick_kernel,
        out_shape=jax.ShapeDtypeStruct(numbers.shape, F32),
        cost_estimate=pl.CostEstimate(flops=2 * 10**9, bytes_accessed=2**21, transcendentals=0),
        compiler_params=pltpu.CompilerParams(vmem_limit_bytes=16 * 2**20),
        name="pick",
    )(jnp.asarray(pick_table()), grads, numbers)


def block_of(grads_ref, chip, core, step, parts, columns):
    first = (2 * lax.rem(chip + step, parts) + core) * columns
    return grads_ref[:, pl.ds(pl.multiple_of(first, LANES), columns)].astype(F32)


def widen_kernel(at_ref, grads_ref, other_ref):
    parts, _, columns = other_ref.shape
    for step in range(parts):
        other_ref[step] = block_of(grads_ref, at_ref[0], 1 - at_ref[1], step, parts, columns)


def widen(at, grads, parts):
    rows, columns = grads.shape
    return pl.pallas_call(
        widen_kernel,
        in_specs=[pl.BlockSpec(memory_space=pltpu.SMEM), pl.BlockSpec(memory_space=pltpu.VMEM)],
        out_shape=jax.ShapeDtypeStruct((parts, rows, columns // (2 * parts)), F32),
        cost_estimate=pl.CostEstimate(flops=10**6, bytes_accessed=3 * 2**20, transcendentals=0),
        compiler_params=pltpu.CompilerParams(vmem_limit_bytes=16 * 2**20),
        name="widen",
    )(at, grads)


def add_kernel(at_ref, grads_ref, arrived_ref, *total_refs):
    parts, _, columns = arrived_ref.shape
    for step, total_ref in enumerate(total_refs):
        total_ref[...] = block_of(grads_ref, at_ref[0], at_ref[1], step, parts, columns) + arrived_ref[step]


def add_own(at, grads, arrived):
    parts, rows, columns = arrived.shape
    vmem = pl.BlockSpec(memory_space=pltpu.VMEM)
    return pl.pallas_call(
        add_kernel,
        in_specs=[pl.BlockSpec(memory_space=pltpu.SMEM), vmem, vmem],
        out_shape=[jax.ShapeDtypeStruct((rows, columns), F32)] * parts,
        cost_estimate=pl.CostEstimate(flops=10**6, bytes_accessed=5 * 2**20, transcendentals=0),
        compiler_params=pltpu.CompilerParams(vmem_limit_bytes=16 * 2**20),
        name="add_own",
    )(at, grads, arrived)


def parts_of(numbers, values):
    numbers = numbers.astype(jnp.int32)
    high = values.astype(BF16).astype(F32)
    return (numbers >> 6).astype(F32), (numbers & 63).astype(F32), high, values - high


SLAB = 16


def one_hots(row, column, high, low):
    row, column, high, low = (jnp.broadcast_to(part, (SLAB, LANES)).astype(BF16) for part in (row, column, high, low))
    counter = lax.broadcasted_iota(jnp.int32, (SLAB, LANES), 0).astype(F32).astype(BF16)
    counters = [counter + jnp.asarray(first, BF16) for first in range(0, TILE, SLAB)]
    zero, one = jnp.zeros((SLAB, LANES), BF16), jnp.ones((SLAB, LANES), BF16)
    at_row = [row == counter for counter in counters]
    weighted = [jnp.where(at, part, zero) for part in (high, low) for at in at_row]
    return jnp.concatenate(weighted, 0), jnp.concatenate([jnp.where(column == at, one, zero) for at in counters], 0)


NT = (((1,), (1,)), ((), ()))


def back(tiles, tall, wide):
    count = len(tiles)
    high, low = halves(jnp.concatenate(tiles, 0))
    both = jnp.dot(jnp.concatenate([high, low], 0), wide[:WIDE], preferred_element_type=F32)
    half = both[: TILE * count] + both[TILE * count :] + jnp.dot(high, wide[WIDE:], preferred_element_type=F32)
    high, low = halves(half)
    out = []
    for first in range(0, TILE * count, TILE):
        part = slice(first, first + TILE)
        out.append(jnp.dot(tall, jnp.concatenate([high[part], high[part], low[part]], 0), preferred_element_type=F32))
    return out


def by_tile(block):
    lane_part = lax.broadcasted_iota(jnp.int32, block[0].shape, 1) // KEPT
    tiles = []
    for tile in range(GROUP):
        moved = [pltpu.roll(block[p], (KEPT * (p - tile)) % LANES, 1) if p != tile else block[p] for p in range(GROUP)]
        total = moved[0]
        for part in range(1, GROUP):
            total = jnp.where(lane_part == part, moved[part], total)
        tiles.append(total)
    return tiles


def scattered(rows_ref, count):
    made = [one_hots(*(rows_ref[part, row : row + 1, :] for part in range(4))) for row in range(count)]
    total = lax.dot_general(
        jnp.concatenate([left for left, _ in made], 1),
        jnp.concatenate([right for _, right in made], 1),
        NT,
        preferred_element_type=F32,
    )
    return total[:TILE] + total[TILE:]


def dense_group(sent_ref, rows_ref, group, firsts, replicas):
    count = replicas // GROUP
    for run, first in enumerate(firsts):

        def rows(offset):
            starts = [first + part * SLAB + offset for part in range(GROUP)]
            return by_tile([sent_ref[pl.ds(start, count, stride=GROUP * SLAB), :] for start in starts])

        values, numbers = rows(group), rows(SLAB // 2 + group)
        for tile in range(GROUP):
            for part, value in enumerate(parts_of(numbers[tile], values[tile])):
                rows_ref[group % 2, tile, part, run * count : (run + 1) * count, :] = value
    tiles = [scattered(rows_ref.at[group % 2, tile], count * len(firsts)) for tile in range(GROUP)]
    return jnp.concatenate(tiles, 1)


def near_kernel(sent_ref, dense_ref, rows_ref):
    for group in range(dense_ref.shape[1] // WIDE):
        columns = slice(group * WIDE, (group + 1) * WIDE)
        dense_ref[:, columns] = dense_group(sent_ref, rows_ref, group, [0], sent_ref.shape[0] // SLAB)


def near(sent, columns):
    return pl.pallas_call(
        near_kernel,
        out_shape=jax.ShapeDtypeStruct((TILE, columns), F32),
        scratch_shapes=[pltpu.VMEM((2, GROUP, 4, SLAB, LANES), F32)],
        compiler_params=pltpu.CompilerParams(vmem_limit_bytes=16 * 2**20),
        cost_estimate=pl.CostEstimate(flops=10**9, bytes_accessed=2**20, transcendentals=0),
        name="near",
    )(sent.reshape(-1, LANES))


def spread_kernel(at_ref, tall_ref, wide_ref, sent_ref, near_ref, update_ref, rows_ref):
    length = sent_ref.shape[0] // FAR_RUNS
    firsts = [pl.multiple_of(lax.rem(at_ref[0] + step, FAR_RUNS) * length, SLAB) for step in range(1, FAR_RUNS)]
    dense = []
    for group in range(near_ref.shape[1] // WIDE):
        columns = slice(group * WIDE, (group + 1) * WIDE)
        dense.append(near_ref[:, columns] + dense_group(sent_ref, rows_ref, group, firsts, length // SLAB))
    for group, piece in enumerate(back(dense, tall_ref[...], wide_ref[...])):
        update_ref[:, group * WIDE : (group + 1) * WIDE] = piece


def spread(at, sent, dense):
    vmem = pl.BlockSpec(memory_space=pltpu.VMEM)
    return pl.pallas_call(
        spread_kernel,
        in_specs=[pl.BlockSpec(memory_space=pltpu.SMEM)] + [vmem] * 4,
        out_shape=jax.ShapeDtypeStruct(dense.shape, F32),
        scratch_shapes=[pltpu.VMEM((2, GROUP, 4, SLAB, LANES), F32)],
        compiler_params=pltpu.CompilerParams(vmem_limit_bytes=16 * 2**20),
        cost_estimate=pl.CostEstimate(flops=2 * 10**9, bytes_accessed=2**20, transcendentals=0),
        name="spread",
    )(at, jnp.asarray(tall_table()), jnp.asarray(wide_table()), sent.reshape(-1, LANES), dense)


def shared_kernel(tall_ref, wide_ref, values_ref, numbers_ref, momentum_ref, left_ref):
    lane_tile = lax.broadcasted_iota(jnp.int32, (1, LANES), 1) // KEPT
    tiles = []
    for group in range(values_ref.shape[0]):
        row, column, high, low = parts_of(numbers_ref[group : group + 1, :], values_ref[group : group + 1, :])
        weighted, hot = one_hots(row, column, high, low)
        hot = jnp.concatenate([jnp.where(lane_tile == tile, hot, jnp.zeros((), BF16)) for tile in range(GROUP)], 0)
        dense = lax.dot_general(weighted, hot, NT, preferred_element_type=F32)
        tiles.append(dense[:TILE] + dense[TILE:])
    for group, piece in enumerate(back(tiles, tall_ref[...], wide_ref[...])):
        columns = slice(group * WIDE, (group + 1) * WIDE)
        left_ref[:, columns] = BETA_DECAY * momentum_ref[:, columns] - piece


def shared(values, numbers, momentum):
    return pl.pallas_call(
        shared_kernel,
        out_shape=jax.ShapeDtypeStruct(momentum.shape, F32),
        compiler_params=pltpu.CompilerParams(vmem_limit_bytes=32 * 2**20),
        cost_estimate=pl.CostEstimate(flops=4 * 10**8, bytes_accessed=2**20, transcendentals=0),
        name="shared",
    )(jnp.asarray(tall_table()), jnp.asarray(wide_table()), values, numbers, momentum)


FSDP = ("x", "core")


def copies_to(block, axis):
    count = lax.axis_size(axis)
    return lax.all_to_all(jnp.broadcast_to(block[None], (count,) + block.shape), axis, 0, 0, tiled=True)


def on_device(partial_grads, momentum_old, indices):
    groups = indices.shape[2] // GROUP
    grads, momentum = partial_grads[0, 0], momentum_old[0]
    chips = lax.axis_size("x")
    at = jnp.stack([lax.axis_index("x"), lax.axis_index("core")]).astype(jnp.int32)
    own_numbers = indices.reshape(groups, LANES)
    numbers = copies_to(own_numbers, FSDP)
    other = widen(at, grads, chips)
    own_part = pick_own(momentum, own_numbers)
    numbers, other, own_part = lax.optimization_barrier((numbers, other, own_part))
    arrived = lax.ppermute(other, "core", [(0, 1), (1, 0)])
    values = pick(grads, numbers)
    values = lax.all_to_all(values, FSDP, 0, 0, tiled=True)
    chip_sums = add_own(at, grads, arrived)
    values, chip_sums = lax.optimization_barrier((values, chip_sums))
    selected = jnp.sum(values, axis=0) + own_part
    own = jnp.concatenate(
        [jnp.pad(part, ((0, SLAB // 2 - groups), (0, 0))) for part in (selected, own_numbers.astype(F32))], 0
    )
    sent = copies_to(own, "z")
    parts = [chip_sums[0]]
    for step in (2, 1, 3):
        parts.append(lax.ppermute(chip_sums[step], "x", [(i, (i + step) % chips) for i in range(chips)]))
    left = shared(selected, own_numbers, momentum)
    sent, left = lax.optimization_barrier((sent, left))
    far = copies_to(sent, "y")
    dense = near(sent, momentum.shape[1])
    far, dense = lax.optimization_barrier((far, dense))
    update = spread(lax.axis_index("y").astype(jnp.int32)[None], far, dense)
    return (left + sum(parts))[None], update


def solution(mesh):
    fine = jax.sharding.Mesh(mesh.devices.reshape(4, 16, 4, 2), ("y", "z", "x", "core"))
    rep = ("y", "z")
    in_specs = (P(rep, FSDP, None, None), P(rep, None, FSDP), P(rep, None, FSDP, None))
    out_specs = (P(rep, None, FSDP), P(None, FSDP))
    return jax.shard_map(on_device, mesh=fine, in_specs=in_specs, out_specs=out_specs, check_vma=False)
```

```python
import functools

import jax
import jax.numpy as jnp
import ml_dtypes
import numpy as np
from jax import lax
from jax.experimental import pallas as pl
from jax.experimental.pallas import tpu as pltpu
from jax.sharding import PartitionSpec as P

TILE = 64
KEPT = 32
LANES = 128
GROUP = LANES // KEPT
WIDE = GROUP * TILE
BETA_DECAY = 0.999
FAR_RUNS = 4
F32 = jnp.float32
BF16 = jnp.bfloat16


def split_table(table):
    high = table.astype(ml_dtypes.bfloat16)
    low = (table - high.astype(np.float64)).astype(ml_dtypes.bfloat16)
    return high, low


def dct_cosines():
    counter = np.arange(TILE)
    scales = np.where(counter == 0, np.sqrt(1.0 / TILE), np.sqrt(2.0 / TILE))
    return scales[:, None] * np.cos(np.pi * (counter[None, :] + 0.5) * counter[:, None] / TILE)


def pick_table():
    high, low = split_table(dct_cosines().T)
    zero = np.zeros_like(high)
    return np.block([[high, zero], [low, zero], [zero, high], [zero, low]])


def wide_table():
    high, low = split_table(dct_cosines())
    eye = np.eye(GROUP)
    return np.concatenate([np.kron(eye, high.astype(np.float32)), np.kron(eye, low.astype(np.float32))], 0).astype(
        ml_dtypes.bfloat16
    )


def tall_table():
    high, low = split_table(dct_cosines().T)
    return np.concatenate([high, low, high], 1)


def halves(value):
    high = value.astype(BF16)
    return high, (value - high.astype(F32)).astype(BF16)


def cosine_rows(table, row):
    counter = lax.broadcasted_iota(jnp.int32, (TILE, LANES), 0)
    hot = jnp.concatenate([counter == (row >> 6), counter == (row & 63)], 0)
    both = jnp.dot(table, jnp.where(hot, 1.0, 0.0).astype(BF16), preferred_element_type=F32)
    down = both[:TILE] + both[TILE : 2 * TILE]
    own = (lax.broadcasted_iota(jnp.int32, (WIDE, LANES), 0) // TILE) == (
        lax.broadcasted_iota(jnp.int32, (WIDE, LANES), 1) // KEPT
    )
    high = jnp.concatenate([both[2 * TILE : 3 * TILE]] * GROUP, 0)
    low = jnp.concatenate([both[3 * TILE :]] * GROUP, 0)
    high = jnp.where(own, high, 0.0).astype(BF16)
    low = jnp.where(own, low, 0.0).astype(BF16)
    return down, jnp.concatenate([high, low], 1)


def picked(source, down, across):
    mixed = jnp.dot(source, across, preferred_element_type=F32)
    return jnp.sum((mixed[:, :LANES] + mixed[:, LANES:]) * down, axis=0, keepdims=True)


def pick_kernel(table_ref, grads_ref, numbers_ref, momentum_ref, own_numbers_ref, values_ref, own_ref):
    parts, groups, _ = numbers_ref.shape
    for part in range(parts):
        for group in range(groups):
            first = (part * groups + group) * WIDE
            down, across = cosine_rows(table_ref[...], numbers_ref[part, group : group + 1, :])
            values_ref[part, group : group + 1, :] = picked(grads_ref[:, first : first + WIDE], down, across)
    for group in range(groups):
        down, across = cosine_rows(table_ref[...], own_numbers_ref[group : group + 1, :])
        high, low = halves(momentum_ref[:, group * WIDE : (group + 1) * WIDE])
        own_ref[group : group + 1, :] = BETA_DECAY * (picked(high, down, across) + picked(low, down, across))


def pick(grads, numbers, momentum, own_numbers):
    return pl.pallas_call(
        pick_kernel,
        out_shape=[jax.ShapeDtypeStruct(numbers.shape, F32), jax.ShapeDtypeStruct(own_numbers.shape, F32)],
        cost_estimate=pl.CostEstimate(flops=2 * 10**9, bytes_accessed=2**21, transcendentals=0),
        compiler_params=pltpu.CompilerParams(vmem_limit_bytes=16 * 2**20),
        name="pick",
    )(jnp.asarray(pick_table()), grads, numbers, momentum, own_numbers)


def block_of(grads_ref, chip, core, step, parts, columns):
    first = (2 * lax.rem(chip + step, parts) + core) * columns
    return grads_ref[:, pl.ds(pl.multiple_of(first, LANES), columns)].astype(F32)


def widen_kernel(at_ref, grads_ref, other_ref):
    parts, _, columns = other_ref.shape
    for step in range(parts):
        other_ref[step] = block_of(grads_ref, at_ref[0], 1 - at_ref[1], step, parts, columns)


def widen(at, grads, parts):
    rows, columns = grads.shape
    return pl.pallas_call(
        widen_kernel,
        in_specs=[pl.BlockSpec(memory_space=pltpu.SMEM), pl.BlockSpec(memory_space=pltpu.VMEM)],
        out_shape=jax.ShapeDtypeStruct((parts, rows, columns // (2 * parts)), F32),
        cost_estimate=pl.CostEstimate(flops=10**6, bytes_accessed=3 * 2**20, transcendentals=0),
        compiler_params=pltpu.CompilerParams(vmem_limit_bytes=16 * 2**20),
        name="widen",
    )(at, grads)


def add_kernel(at_ref, grads_ref, arrived_ref, *total_refs):
    parts, _, columns = arrived_ref.shape
    for step, total_ref in enumerate(total_refs):
        total_ref[...] = block_of(grads_ref, at_ref[0], at_ref[1], step, parts, columns) + arrived_ref[step]


def add_own(at, grads, arrived):
    parts, rows, columns = arrived.shape
    vmem = pl.BlockSpec(memory_space=pltpu.VMEM)
    return pl.pallas_call(
        add_kernel,
        in_specs=[pl.BlockSpec(memory_space=pltpu.SMEM), vmem, vmem],
        out_shape=[jax.ShapeDtypeStruct((rows, columns), F32)] * parts,
        cost_estimate=pl.CostEstimate(flops=10**6, bytes_accessed=5 * 2**20, transcendentals=0),
        compiler_params=pltpu.CompilerParams(vmem_limit_bytes=16 * 2**20),
        name="add_own",
    )(at, grads, arrived)


def parts_of(numbers, values):
    numbers = numbers.astype(jnp.int32)
    high = values.astype(BF16).astype(F32)
    return (numbers >> 6).astype(F32), (numbers & 63).astype(F32), high, values - high


SLAB = 16


def one_hots(row, column, high, low):
    row, column, high, low = (jnp.broadcast_to(part, (SLAB, LANES)).astype(BF16) for part in (row, column, high, low))
    counter = lax.broadcasted_iota(jnp.int32, (SLAB, LANES), 0).astype(F32).astype(BF16)
    counters = [counter + jnp.asarray(first, BF16) for first in range(0, TILE, SLAB)]
    zero, one = jnp.zeros((SLAB, LANES), BF16), jnp.ones((SLAB, LANES), BF16)
    at_row = [row == counter for counter in counters]
    weighted = [jnp.where(at, part, zero) for part in (high, low) for at in at_row]
    return jnp.concatenate(weighted, 0), jnp.concatenate([jnp.where(column == at, one, zero) for at in counters], 0)


NT = (((1,), (1,)), ((), ()))


def back(tiles, tall, wide):
    count = len(tiles)
    high, low = halves(jnp.concatenate(tiles, 0))
    both = jnp.dot(jnp.concatenate([high, low], 0), wide[:WIDE], preferred_element_type=F32)
    half = both[: TILE * count] + both[TILE * count :] + jnp.dot(high, wide[WIDE:], preferred_element_type=F32)
    high, low = halves(half)
    out = []
    for first in range(0, TILE * count, TILE):
        part = slice(first, first + TILE)
        out.append(jnp.dot(tall, jnp.concatenate([high[part], high[part], low[part]], 0), preferred_element_type=F32))
    return out


def by_tile(block):
    lane_part = lax.broadcasted_iota(jnp.int32, block[0].shape, 1) // KEPT
    tiles = []
    for tile in range(GROUP):
        moved = [pltpu.roll(block[p], (KEPT * (p - tile)) % LANES, 1) if p != tile else block[p] for p in range(GROUP)]
        total = moved[0]
        for part in range(1, GROUP):
            total = jnp.where(lane_part == part, moved[part], total)
        tiles.append(total)
    return tiles


def scattered(rows_ref, count):
    made = [one_hots(*(rows_ref[part, row : row + 1, :] for part in range(4))) for row in range(count)]
    total = lax.dot_general(
        jnp.concatenate([left for left, _ in made], 1),
        jnp.concatenate([right for _, right in made], 1),
        NT,
        preferred_element_type=F32,
    )
    return total[:TILE] + total[TILE:]


def dense_group(sent_ref, rows_ref, group, groups, firsts, replicas):
    count = replicas // GROUP
    for run, first in enumerate(firsts):

        def rows(offset):
            starts = [first + part * 2 * groups + offset for part in range(GROUP)]
            return by_tile([sent_ref[pl.ds(start, count, stride=GROUP * 2 * groups), :] for start in starts])

        values, numbers = rows(group), rows(groups + group)
        for tile in range(GROUP):
            for part, value in enumerate(parts_of(numbers[tile], values[tile])):
                rows_ref[group % 2, tile, part, run * count : (run + 1) * count, :] = value
    tiles = [scattered(rows_ref.at[group % 2, tile], count * len(firsts)) for tile in range(GROUP)]
    return jnp.concatenate(tiles, 1)


def near_kernel(sent_ref, dense_ref, rows_ref):
    groups = dense_ref.shape[1] // WIDE
    for group in range(groups):
        columns = slice(group * WIDE, (group + 1) * WIDE)
        dense_ref[:, columns] = dense_group(sent_ref, rows_ref, group, groups, [0], sent_ref.shape[0] // (2 * groups))


def near(sent, columns):
    return pl.pallas_call(
        near_kernel,
        out_shape=jax.ShapeDtypeStruct((TILE, columns), F32),
        scratch_shapes=[pltpu.VMEM((2, GROUP, 4, SLAB, LANES), F32)],
        compiler_params=pltpu.CompilerParams(vmem_limit_bytes=16 * 2**20),
        cost_estimate=pl.CostEstimate(flops=10**9, bytes_accessed=2**20, transcendentals=0),
        name="near",
    )(sent.reshape(-1, LANES))


def spread_kernel(at_ref, tall_ref, wide_ref, sent_ref, near_ref, update_ref, rows_ref):
    length = sent_ref.shape[0] // FAR_RUNS
    groups = near_ref.shape[1] // WIDE
    firsts = [pl.multiple_of(lax.rem(at_ref[0] + step, FAR_RUNS) * length, 8) for step in range(1, FAR_RUNS)]
    dense = []
    for group in range(groups):
        columns = slice(group * WIDE, (group + 1) * WIDE)
        dense.append(near_ref[:, columns] + dense_group(sent_ref, rows_ref, group, groups, firsts, length // (2 * groups)))
    for group, piece in enumerate(back(dense, tall_ref[...], wide_ref[...])):
        update_ref[:, group * WIDE : (group + 1) * WIDE] = piece


def spread(at, sent, dense):
    vmem = pl.BlockSpec(memory_space=pltpu.VMEM)
    return pl.pallas_call(
        spread_kernel,
        in_specs=[pl.BlockSpec(memory_space=pltpu.SMEM)] + [vmem] * 4,
        out_shape=jax.ShapeDtypeStruct(dense.shape, F32),
        scratch_shapes=[pltpu.VMEM((2, GROUP, 4, SLAB, LANES), F32)],
        compiler_params=pltpu.CompilerParams(vmem_limit_bytes=16 * 2**20),
        cost_estimate=pl.CostEstimate(flops=2 * 10**9, bytes_accessed=2**20, transcendentals=0),
        name="spread",
    )(at, jnp.asarray(tall_table()), jnp.asarray(wide_table()), sent.reshape(-1, LANES), dense)


def shared_kernel(tall_ref, wide_ref, values_ref, numbers_ref, momentum_ref, left_ref):
    lane_tile = lax.broadcasted_iota(jnp.int32, (1, LANES), 1) // KEPT
    tiles = []
    for group in range(values_ref.shape[0]):
        row, column, high, low = parts_of(numbers_ref[group : group + 1, :], values_ref[group : group + 1, :])
        weighted, hot = one_hots(row, column, high, low)
        hot = jnp.concatenate([jnp.where(lane_tile == tile, hot, jnp.zeros((), BF16)) for tile in range(GROUP)], 0)
        dense = lax.dot_general(weighted, hot, NT, preferred_element_type=F32)
        tiles.append(dense[:TILE] + dense[TILE:])
    for group, piece in enumerate(back(tiles, tall_ref[...], wide_ref[...])):
        columns = slice(group * WIDE, (group + 1) * WIDE)
        left_ref[:, columns] = BETA_DECAY * momentum_ref[:, columns] - piece


def shared(values, numbers, momentum):
    return pl.pallas_call(
        shared_kernel,
        out_shape=jax.ShapeDtypeStruct(momentum.shape, F32),
        compiler_params=pltpu.CompilerParams(vmem_limit_bytes=32 * 2**20),
        cost_estimate=pl.CostEstimate(flops=4 * 10**8, bytes_accessed=2**20, transcendentals=0),
        name="shared",
    )(jnp.asarray(tall_table()), jnp.asarray(wide_table()), values, numbers, momentum)


FSDP = ("x", "core")


def copies_to(block, axis):
    count = lax.axis_size(axis)
    return lax.all_to_all(jnp.broadcast_to(block[None], (count,) + block.shape), axis, 0, 0, tiled=True)


def on_device(partial_grads, momentum_old, indices):
    groups = indices.shape[2] // GROUP
    grads, momentum = partial_grads[0, 0], momentum_old[0]
    chips = lax.axis_size("x")
    at = jnp.stack([lax.axis_index("x"), lax.axis_index("core")]).astype(jnp.int32)
    own_numbers = indices.reshape(groups, LANES)
    numbers = copies_to(own_numbers, FSDP)
    other = widen(at, grads, chips)
    numbers, other = lax.optimization_barrier((numbers, other))
    arrived = lax.ppermute(other, "core", [(0, 1), (1, 0)])
    values, own_part = pick(grads, numbers, momentum, own_numbers)
    values = lax.all_to_all(values, FSDP, 0, 0, tiled=True)
    chip_sums = add_own(at, grads, arrived)
    values, chip_sums = lax.optimization_barrier((values, chip_sums))
    selected = jnp.sum(values, axis=0) + own_part
    own = jnp.concatenate([selected, own_numbers.astype(F32)], 0).reshape(1, -1)
    sent = copies_to(own, "z")
    parts = [chip_sums[0]]
    for step in (2, 1, 3):
        parts.append(lax.ppermute(chip_sums[step], "x", [(i, (i + step) % chips) for i in range(chips)]))
    left = shared(selected, own_numbers, momentum)
    sent, left = lax.optimization_barrier((sent, left))
    far = copies_to(sent.reshape(1, -1), "y")
    dense = near(sent, momentum.shape[1])
    far, dense = lax.optimization_barrier((far, dense))
    update = spread(lax.axis_index("y").astype(jnp.int32)[None], far, dense)
    return (left + sum(parts))[None], update


def solution(mesh):
    fine = jax.sharding.Mesh(mesh.devices.reshape(4, 16, 4, 2), ("y", "z", "x", "core"))
    rep = ("y", "z")
    in_specs = (P(rep, FSDP, None, None), P(rep, None, FSDP), P(rep, None, FSDP, None))
    out_specs = (P(rep, None, FSDP), P(None, FSDP))
    return jax.shard_map(on_device, mesh=fine, in_specs=in_specs, out_specs=out_specs, check_vma=False)
```

```python
import functools

import jax
import jax.numpy as jnp
import ml_dtypes
import numpy as np
from jax import lax
from jax.experimental import pallas as pl
from jax.experimental.pallas import tpu as pltpu
from jax.sharding import PartitionSpec as P

TILE = 64
KEPT = 32
LANES = 128
GROUP = LANES // KEPT
WIDE = GROUP * TILE
BETA_DECAY = 0.999
FAR_RUNS = 4
F32 = jnp.float32
BF16 = jnp.bfloat16


def split_table(table):
    high = table.astype(ml_dtypes.bfloat16)
    low = (table - high.astype(np.float64)).astype(ml_dtypes.bfloat16)
    return high, low


def dct_cosines():
    counter = np.arange(TILE)
    scales = np.where(counter == 0, np.sqrt(1.0 / TILE), np.sqrt(2.0 / TILE))
    return scales[:, None] * np.cos(np.pi * (counter[None, :] + 0.5) * counter[:, None] / TILE)


def pick_table():
    high, low = split_table(dct_cosines().T)
    zero = np.zeros_like(high)
    return np.block([[high, zero], [low, zero], [zero, high], [zero, low]])


def wide_table():
    high, low = split_table(dct_cosines())
    eye = np.eye(GROUP)
    return np.concatenate([np.kron(eye, high.astype(np.float32)), np.kron(eye, low.astype(np.float32))], 0).astype(
        ml_dtypes.bfloat16
    )


def tall_table():
    high, low = split_table(dct_cosines().T)
    return np.concatenate([high, low, high], 1)


def halves(value):
    high = value.astype(BF16)
    return high, (value - high.astype(F32)).astype(BF16)


def cosine_rows(table, row):
    counter = lax.broadcasted_iota(jnp.int32, (TILE, LANES), 0)
    hot = jnp.concatenate([counter == (row >> 6), counter == (row & 63)], 0)
    both = jnp.dot(table, jnp.where(hot, 1.0, 0.0).astype(BF16), preferred_element_type=F32)
    down = both[:TILE] + both[TILE : 2 * TILE]
    own = (lax.broadcasted_iota(jnp.int32, (WIDE, LANES), 0) // TILE) == (
        lax.broadcasted_iota(jnp.int32, (WIDE, LANES), 1) // KEPT
    )
    high = jnp.concatenate([both[2 * TILE : 3 * TILE]] * GROUP, 0)
    low = jnp.concatenate([both[3 * TILE :]] * GROUP, 0)
    high = jnp.where(own, high, 0.0).astype(BF16)
    low = jnp.where(own, low, 0.0).astype(BF16)
    return down, jnp.concatenate([high, low], 1)


def picked(source, down, across):
    mixed = jnp.dot(source, across, preferred_element_type=F32)
    return jnp.sum((mixed[:, :LANES] + mixed[:, LANES:]) * down, axis=0, keepdims=True)


def pick_kernel(table_ref, grads_ref, numbers_ref, momentum_ref, own_numbers_ref, values_ref, own_ref):
    parts, groups, _ = numbers_ref.shape
    for part in range(parts):
        for group in range(groups):
            first = (part * groups + group) * WIDE
            down, across = cosine_rows(table_ref[...], numbers_ref[part, group : group + 1, :])
            values_ref[part, group : group + 1, :] = picked(grads_ref[:, first : first + WIDE], down, across)
    for group in range(groups):
        down, across = cosine_rows(table_ref[...], own_numbers_ref[group : group + 1, :])
        high, low = halves(momentum_ref[:, group * WIDE : (group + 1) * WIDE])
        own_ref[group : group + 1, :] = BETA_DECAY * (picked(high, down, across) + picked(low, down, across))


def pick(grads, numbers, momentum, own_numbers):
    return pl.pallas_call(
        pick_kernel,
        out_shape=[jax.ShapeDtypeStruct(numbers.shape, F32), jax.ShapeDtypeStruct(own_numbers.shape, F32)],
        cost_estimate=pl.CostEstimate(flops=2 * 10**9, bytes_accessed=2**21, transcendentals=0),
        compiler_params=pltpu.CompilerParams(vmem_limit_bytes=16 * 2**20),
        name="pick",
    )(jnp.asarray(pick_table()), grads, numbers, momentum, own_numbers)


def block_of(grads_ref, chip, core, step, parts, columns):
    first = (2 * lax.rem(chip + step, parts) + core) * columns
    return grads_ref[:, pl.ds(pl.multiple_of(first, LANES), columns)].astype(F32)


def widen_kernel(at_ref, grads_ref, other_ref):
    parts, _, columns = other_ref.shape
    for step in range(parts):
        other_ref[step] = block_of(grads_ref, at_ref[0], 1 - at_ref[1], step, parts, columns)


def widen(at, grads, parts):
    rows, columns = grads.shape
    return pl.pallas_call(
        widen_kernel,
        in_specs=[pl.BlockSpec(memory_space=pltpu.SMEM), pl.BlockSpec(memory_space=pltpu.VMEM)],
        out_shape=jax.ShapeDtypeStruct((parts, rows, columns // (2 * parts)), F32),
        cost_estimate=pl.CostEstimate(flops=10**6, bytes_accessed=3 * 2**20, transcendentals=0),
        compiler_params=pltpu.CompilerParams(vmem_limit_bytes=16 * 2**20),
        name="widen",
    )(at, grads)


def add_kernel(at_ref, grads_ref, arrived_ref, *total_refs):
    parts, _, columns = arrived_ref.shape
    for step, total_ref in enumerate(total_refs):
        total_ref[...] = block_of(grads_ref, at_ref[0], at_ref[1], step, parts, columns) + arrived_ref[step]


def add_own(at, grads, arrived):
    parts, rows, columns = arrived.shape
    vmem = pl.BlockSpec(memory_space=pltpu.VMEM)
    return pl.pallas_call(
        add_kernel,
        in_specs=[pl.BlockSpec(memory_space=pltpu.SMEM), vmem, vmem],
        out_shape=[jax.ShapeDtypeStruct((rows, columns), F32)] * parts,
        cost_estimate=pl.CostEstimate(flops=10**6, bytes_accessed=5 * 2**20, transcendentals=0),
        compiler_params=pltpu.CompilerParams(vmem_limit_bytes=16 * 2**20),
        name="add_own",
    )(at, grads, arrived)


def parts_of(numbers, values):
    numbers = numbers.astype(jnp.int32)
    high = values.astype(BF16).astype(F32)
    return (numbers >> 6).astype(F32), (numbers & 63).astype(F32), high, values - high


SLAB = 16


def one_hots(row, column, high, low):
    row, column, high, low = (jnp.broadcast_to(part, (SLAB, LANES)).astype(BF16) for part in (row, column, high, low))
    counter = lax.broadcasted_iota(jnp.int32, (SLAB, LANES), 0).astype(F32).astype(BF16)
    counters = [counter + jnp.asarray(first, BF16) for first in range(0, TILE, SLAB)]
    zero, one = jnp.zeros((SLAB, LANES), BF16), jnp.ones((SLAB, LANES), BF16)
    at_row = [row == counter for counter in counters]
    weighted = [jnp.where(at, part, zero) for part in (high, low) for at in at_row]
    return jnp.concatenate(weighted, 0), jnp.concatenate([jnp.where(column == at, one, zero) for at in counters], 0)


NT = (((1,), (1,)), ((), ()))


def back(tiles, tall, wide):
    count = len(tiles)
    high, low = halves(jnp.concatenate(tiles, 0))
    both = jnp.dot(jnp.concatenate([high, low], 0), wide[:WIDE], preferred_element_type=F32)
    half = both[: TILE * count] + both[TILE * count :] + jnp.dot(high, wide[WIDE:], preferred_element_type=F32)
    high, low = halves(half)
    out = []
    for first in range(0, TILE * count, TILE):
        part = slice(first, first + TILE)
        out.append(jnp.dot(tall, jnp.concatenate([high[part], high[part], low[part]], 0), preferred_element_type=F32))
    return out


def by_tile(block):
    lane_part = lax.broadcasted_iota(jnp.int32, block[0].shape, 1) // KEPT
    tiles = []
    for tile in range(GROUP):
        moved = [pltpu.roll(block[p], (KEPT * (p - tile)) % LANES, 1) if p != tile else block[p] for p in range(GROUP)]
        total = moved[0]
        for part in range(1, GROUP):
            total = jnp.where(lane_part == part, moved[part], total)
        tiles.append(total)
    return tiles


def scattered(rows_ref, count):
    made = [one_hots(*(rows_ref[part, row : row + 1, :] for part in range(4))) for row in range(count)]
    total = lax.dot_general(
        jnp.concatenate([left for left, _ in made], 1),
        jnp.concatenate([right for _, right in made], 1),
        NT,
        preferred_element_type=F32,
    )
    return total[:TILE] + total[TILE:]


def dense_group(sent_ref, rows_ref, group, groups, firsts, replicas):
    count = replicas // GROUP
    for run, first in enumerate(firsts):

        def rows(offset):
            starts = [first + part * 2 * groups + offset for part in range(GROUP)]
            return by_tile([sent_ref[pl.ds(start, count, stride=GROUP * 2 * groups), :] for start in starts])

        values, numbers = rows(group), rows(groups + group)
        for tile in range(GROUP):
            for part, value in enumerate(parts_of(numbers[tile], values[tile])):
                rows_ref[group % 2, tile, part, run * count : (run + 1) * count, :] = value
    tiles = [scattered(rows_ref.at[group % 2, tile], count * len(firsts)) for tile in range(GROUP)]
    return jnp.concatenate(tiles, 1)


def near_kernel(sent_ref, dense_ref, rows_ref):
    groups = dense_ref.shape[1] // WIDE
    for group in range(groups):
        columns = slice(group * WIDE, (group + 1) * WIDE)
        dense_ref[:, columns] = dense_group(sent_ref, rows_ref, group, groups, [0], sent_ref.shape[0] // (2 * groups))


def near(sent, columns):
    return pl.pallas_call(
        near_kernel,
        out_shape=jax.ShapeDtypeStruct((TILE, columns), F32),
        scratch_shapes=[pltpu.VMEM((2, GROUP, 4, SLAB, LANES), F32)],
        compiler_params=pltpu.CompilerParams(vmem_limit_bytes=16 * 2**20),
        cost_estimate=pl.CostEstimate(flops=10**9, bytes_accessed=2**20, transcendentals=0),
        name="near",
    )(sent.reshape(-1, LANES))


def spread_kernel(at_ref, tall_ref, wide_ref, sent_ref, near_ref, update_ref, rows_ref):
    length = sent_ref.shape[0] // FAR_RUNS
    groups = near_ref.shape[1] // WIDE
    firsts = [pl.multiple_of(lax.rem(at_ref[0] + step, FAR_RUNS) * length, 8) for step in range(1, FAR_RUNS)]
    dense = []
    for group in range(groups):
        columns = slice(group * WIDE, (group + 1) * WIDE)
        dense.append(near_ref[:, columns] + dense_group(sent_ref, rows_ref, group, groups, firsts, length // (2 * groups)))
    for group, piece in enumerate(back(dense, tall_ref[...], wide_ref[...])):
        update_ref[:, group * WIDE : (group + 1) * WIDE] = piece


def spread(at, sent, dense):
    vmem = pl.BlockSpec(memory_space=pltpu.VMEM)
    return pl.pallas_call(
        spread_kernel,
        in_specs=[pl.BlockSpec(memory_space=pltpu.SMEM)] + [vmem] * 4,
        out_shape=jax.ShapeDtypeStruct(dense.shape, F32),
        scratch_shapes=[pltpu.VMEM((2, GROUP, 4, SLAB, LANES), F32)],
        compiler_params=pltpu.CompilerParams(vmem_limit_bytes=16 * 2**20),
        cost_estimate=pl.CostEstimate(flops=2 * 10**9, bytes_accessed=2**20, transcendentals=0),
        name="spread",
    )(at, jnp.asarray(tall_table()), jnp.asarray(wide_table()), sent.reshape(-1, LANES), dense)


def shared_kernel(tall_ref, wide_ref, values_ref, numbers_ref, momentum_ref, left_ref):
    lane_tile = lax.broadcasted_iota(jnp.int32, (1, LANES), 1) // KEPT
    tiles = []
    for group in range(values_ref.shape[0]):
        row, column, high, low = parts_of(numbers_ref[group : group + 1, :], values_ref[group : group + 1, :])
        weighted, hot = one_hots(row, column, high, low)
        hot = jnp.concatenate([jnp.where(lane_tile == tile, hot, jnp.zeros((), BF16)) for tile in range(GROUP)], 0)
        dense = lax.dot_general(weighted, hot, NT, preferred_element_type=F32)
        tiles.append(dense[:TILE] + dense[TILE:])
    for group, piece in enumerate(back(tiles, tall_ref[...], wide_ref[...])):
        columns = slice(group * WIDE, (group + 1) * WIDE)
        left_ref[:, columns] = BETA_DECAY * momentum_ref[:, columns] - piece


def shared(values, numbers, momentum):
    return pl.pallas_call(
        shared_kernel,
        out_shape=jax.ShapeDtypeStruct(momentum.shape, F32),
        compiler_params=pltpu.CompilerParams(vmem_limit_bytes=32 * 2**20),
        cost_estimate=pl.CostEstimate(flops=4 * 10**8, bytes_accessed=2**20, transcendentals=0),
        name="shared",
    )(jnp.asarray(tall_table()), jnp.asarray(wide_table()), values, numbers, momentum)


FSDP = ("x", "core")


def copies_to(block, axis):
    count = lax.axis_size(axis)
    return lax.all_to_all(jnp.broadcast_to(block[None], (count,) + block.shape), axis, 0, 0, tiled=True)


def on_device(partial_grads, momentum_old, indices):
    groups = indices.shape[2] // GROUP
    grads, momentum = partial_grads[0, 0], momentum_old[0]
    chips = lax.axis_size("x")
    at = jnp.stack([lax.axis_index("x"), lax.axis_index("core")]).astype(jnp.int32)
    own_numbers = indices.reshape(groups, LANES)
    numbers = copies_to(own_numbers, FSDP)
    other = widen(at, grads, chips)
    numbers, other = lax.optimization_barrier((numbers, other))
    arrived = lax.ppermute(other, "core", [(0, 1), (1, 0)])
    values, own_part = pick(grads, numbers, momentum, own_numbers)
    values = lax.all_to_all(values, FSDP, 0, 0, tiled=True)
    chip_sums = add_own(at, grads, arrived)
    values, chip_sums = lax.optimization_barrier((values, chip_sums))
    selected = jnp.sum(values, axis=0) + own_part
    own = jnp.concatenate([selected, own_numbers.astype(F32)], 0).reshape(1, -1)
    sent = copies_to(own, "z")
    parts = [chip_sums[0]]
    for step in (2, 1, 3):
        parts.append(lax.ppermute(chip_sums[step], "x", [(i, (i + step) % chips) for i in range(chips)]))
    chosen = (own.reshape(-1, LANES)[groups:]).astype(jnp.int32)
    sent, chosen = lax.optimization_barrier((sent, chosen))
    left = shared(selected, chosen, momentum)
    far = copies_to(sent.reshape(1, -1), "y")
    dense = near(sent, momentum.shape[1])
    far, dense = lax.optimization_barrier((far, dense))
    update = spread(lax.axis_index("y").astype(jnp.int32)[None], far, dense)
    return (left + sum(parts))[None], update


def solution(mesh):
    fine = jax.sharding.Mesh(mesh.devices.reshape(4, 16, 4, 2), ("y", "z", "x", "core"))
    rep = ("y", "z")
    in_specs = (P(rep, FSDP, None, None), P(rep, None, FSDP), P(rep, None, FSDP, None))
    out_specs = (P(rep, None, FSDP), P(None, FSDP))
    return jax.shard_map(on_device, mesh=fine, in_specs=in_specs, out_specs=out_specs, check_vma=False)
```
